512 devices in a mesh: doc: 16 (over y, core), seq: 32 (over x, z).
Axes of the slice: x: 4, y: 8, z: 8, core: 2. Of those that a mesh axis runs over, the one named last changes fastest.
Arguments:
- text_query: bfloat16 [65536, 2048], P(('doc', 'seq')), parts along dimension 0, may hold values from -6 to 6
- stretch_kv: bfloat16 [65536, 4, 256], P(('doc', 'seq')), parts along dimension 0, may hold values from -6 to 6
- cache_kv: bfloat16 [4096, 4, 256], P(('doc', 'seq')), parts along dimension 0, may hold values from -6 to 6
- cross_query: bfloat16 [65536, 2048], P(('doc', 'seq')), parts along dimension 0, may hold values from -6 to 6
- image_kv: bfloat16 [512, 32, 4, 256], P(('doc', 'seq')), parts along dimension 0, may hold values from -6 to 6
- image_start: int32 [512], P('doc'), parts along dimension 0, may hold values from 0 to 4095, as said below
- image_stop: int32 [512], P('doc'), parts along dimension 0, may hold values from 1 to 4096, as said below
- image_lengths: int32 [512], P('doc'), parts along dimension 0, may hold values from 2 to 32
- cross_gate: float32 [16], P('doc'), parts along dimension 0, may hold values from 0.5 to 2
Outputs:
- self_context: bfloat16 [65536, 2048], P(('doc', 'seq')), parts along dimension 0
- cross_context: bfloat16 [65536, 2048], P(('doc', 'seq')), parts along dimension 0
The draws below stay inside these ranges and needn't reach their ends.
There are 16 independent parts, one for each index of `doc`. The reference program is written for one: setup_inputs(seed, part) draws one part's arguments, and reference() takes and returns one part's arrays. A program takes and returns all parts, laid end to end along the dimension named above; each array names one. Nothing has to cross between parts.
Inputs may be any that keep to these rules, and one draw needn't show every extreme that they name: `image_start`: image i's span starts in rows i * 128 to (i + 1) * 128 - 1; image 0 starts at row 0. image_stop[i] > image_start[i] and image_stop[i] <= min((i + 2) * 128, 4096); the last image's span ends at 4096.
All inputs are finite; a program needn't handle non-finite values.
Results may differ from the reference program's by a relative error of at most 0.0049.
Values may be sent and summed in bfloat16 or wider, within the bound.
No kernel may reach another device: no remote copies, remote signals or barrier semaphores. Data moves between devices by JAX's collectives and lax.ppermute only.
A program may use at most 64 MiB of HBM per device.

```python
import math
import jax
import jax.numpy as jnp
from jax import lax

H = 16
G = 4
HD = 128
TOK_DEV = 128
IMG_TOK = 32
TOKENS = 4096
CACHE = 256
NIMG = 32


def span_table(key):
    key = jax.random.fold_in(key, 5)
    first_key, second_key = jax.random.split(key)
    offsets = jax.random.randint(first_key, (NIMG,), 0, TOK_DEV).astype(jnp.int32)
    offsets = offsets.at[0].set(0)
    starts = jnp.arange(NIMG, dtype=jnp.int32) * TOK_DEV + offsets
    extra = jax.random.randint(second_key, (NIMG,), 0, 2 * TOK_DEV - offsets).astype(jnp.int32)
    stops = jnp.minimum(starts + 1 + extra, TOKENS)
    stops = stops.at[NIMG - 1].set(TOKENS)
    return (starts, stops)


def draw_text_query(key, part):
    key = jax.random.fold_in(key, 11)
    field = jnp.clip(jax.random.normal(key, (TOKENS, H * HD), jnp.float32), -6.0, 6.0)
    return field.astype(jnp.bfloat16)


def draw_stretch_kv(key, part):
    key = jax.random.fold_in(key, 13)
    field = jnp.clip(jax.random.normal(key, (TOKENS, G, 2 * HD), jnp.float32), -6.0, 6.0)
    return field.astype(jnp.bfloat16)


def draw_cache_kv(key, part):
    key = jax.random.fold_in(key, 17)
    field = jnp.clip(jax.random.normal(key, (CACHE, G, 2 * HD), jnp.float32), -6.0, 6.0)
    return field.astype(jnp.bfloat16)


def draw_cross_query(key, part):
    key = jax.random.fold_in(key, 19)
    field = jnp.clip(jax.random.normal(key, (TOKENS, H * HD), jnp.float32), -6.0, 6.0)
    return field.astype(jnp.bfloat16)


def draw_image_kv(key, part):
    key = jax.random.fold_in(key, 23)
    field = jnp.clip(jax.random.normal(key, (NIMG, IMG_TOK, G, 2 * HD), jnp.float32), -6.0, 6.0)
    return field.astype(jnp.bfloat16)


def draw_image_start(key, part):
    starts, stops = span_table(key)
    return starts


def draw_image_stop(key, part):
    starts, stops = span_table(key)
    return stops


def draw_image_lengths(key, part):
    key = jax.random.fold_in(key, 29)
    first_key, second_key, third_key = jax.random.split(key, 3)
    lengths = jax.random.randint(first_key, (NIMG,), IMG_TOK // 2, IMG_TOK + 1).astype(jnp.int32)
    lowest = jax.random.randint(second_key, (), 0, NIMG)
    highest = (lowest + 1 + jax.random.randint(third_key, (), 0, NIMG - 1)) % NIMG
    lengths = lengths.at[lowest].set(2)
    lengths = lengths.at[highest].set(IMG_TOK)
    return lengths


def setup_inputs(seed: int = 0, part: int = 0) -> dict:
    keys = jax.random.split(jax.random.key(seed), 10)
    part_splits = jax.random.split(jax.random.fold_in(keys[9], part), 10)
    return {
        "text_query": draw_text_query(jax.random.fold_in(jax.random.fold_in(keys[9], part), 71), part),
        "stretch_kv": draw_stretch_kv(jax.random.fold_in(jax.random.fold_in(keys[9], part), 71), part),
        "cache_kv": draw_cache_kv(jax.random.fold_in(jax.random.fold_in(keys[9], part), 71), part),
        "cross_query": draw_cross_query(jax.random.fold_in(jax.random.fold_in(keys[9], part), 71), part),
        "image_kv": draw_image_kv(jax.random.fold_in(jax.random.fold_in(keys[9], part), 71), part),
        "image_start": draw_image_start(jax.random.fold_in(jax.random.fold_in(keys[9], part), 71), part),
        "image_stop": draw_image_stop(jax.random.fold_in(jax.random.fold_in(keys[9], part), 71), part),
        "image_lengths": draw_image_lengths(jax.random.fold_in(jax.random.fold_in(keys[9], part), 71), part),
        "cross_gate": jnp.clip(jax.random.uniform(part_splits[8], (1,), jnp.float32, 0.5, 2.0), 0.5, 2.0),
    }


LOW_SCORE = -1e+30

def normalize(scores, allowed):
    masked = jnp.where(allowed, scores, LOW_SCORE)
    highest = lax.optimization_barrier(jnp.max(masked, axis=-1, keepdims=True))
    weights = jnp.where(allowed, jnp.exp(masked - highest), 0.0)
    present = jnp.any(allowed, axis=-1, keepdims=True)
    totals = lax.optimization_barrier(jnp.sum(weights, axis=-1, keepdims=True)) + jnp.where(present, 0.0, 1.0)
    return ((weights / totals).astype(jnp.bfloat16), present)

def causal_head(queries, key_rows, value_rows, cached):
    token_total = queries.shape[0]
    block_rows = min(token_total, max(512, token_total // 8))
    score_scale = 1.0 / math.sqrt(HD)
    results = []
    for first_row in range(0, token_total, block_rows):
        key_reach = cached + first_row + block_rows
        scores = jnp.dot(queries[first_row:first_row + block_rows], key_rows[:key_reach].T, preferred_element_type=jnp.float32) * score_scale
        columns = jnp.arange(key_reach)[None, :]
        positions = first_row + jnp.arange(block_rows)[:, None]
        weights, present = normalize(scores, (columns < cached) | (columns - cached <= positions))
        results.append(jnp.dot(weights, value_rows[:key_reach], preferred_element_type=jnp.float32).astype(jnp.bfloat16))
    return jnp.concatenate(results, 0)

def reference(text_query, stretch_kv, cache_kv, cross_query, image_kv, image_start, image_stop, image_lengths, cross_gate):
    group_size = H // G
    score_scale = 1.0 / math.sqrt(HD)
    key_rows = jnp.concatenate([cache_kv[:, :, :HD], stretch_kv[:, :, :HD]], 0)
    value_rows = jnp.concatenate([cache_kv[:, :, HD:], stretch_kv[:, :, HD:]], 0)
    heads_first = jnp.transpose(text_query.reshape(TOKENS, H, HD), (1, 0, 2))

    def one_head(head_number):
        group_number = head_number // group_size
        queries = lax.dynamic_index_in_dim(heads_first, head_number, 0, keepdims=False)
        head_keys = lax.dynamic_index_in_dim(key_rows, group_number, 1, keepdims=False)
        head_values = lax.dynamic_index_in_dim(value_rows, group_number, 1, keepdims=False)
        return causal_head(queries, head_keys, head_values, CACHE)
    self_heads = lax.map(one_head, jnp.arange(H, dtype=jnp.int32))
    self_context = jnp.transpose(self_heads, (1, 0, 2)).reshape(TOKENS, H * HD)
    gate_value = jnp.tanh(cross_gate[0])
    zero_entry = jnp.zeros((1,), jnp.int32)
    start_table = jnp.concatenate([zero_entry, image_start.astype(jnp.int32)])
    stop_table = jnp.concatenate([zero_entry, image_stop.astype(jnp.int32)])
    length_table = jnp.concatenate([zero_entry, image_lengths.astype(jnp.int32)])
    image_table = jnp.concatenate([jnp.zeros((1,) + image_kv.shape[1:], image_kv.dtype), image_kv], 0)
    query_blocks = cross_query.reshape(NIMG, TOK_DEV, G, group_size, HD)
    within = jnp.arange(2 * IMG_TOK, dtype=jnp.int32) % IMG_TOK

    def one_block(owner):
        paired = lax.dynamic_slice_in_dim(image_table, owner, 2, 0).reshape(2 * IMG_TOK, G, 2 * HD)
        slot_start = jnp.repeat(lax.dynamic_slice_in_dim(start_table, owner, 2), IMG_TOK)
        slot_stop = jnp.repeat(lax.dynamic_slice_in_dim(stop_table, owner, 2), IMG_TOK)
        slot_length = jnp.repeat(lax.dynamic_slice_in_dim(length_table, owner, 2), IMG_TOK)
        positions = owner * TOK_DEV + jnp.arange(TOK_DEV, dtype=jnp.int32)[:, None]
        allowed = (slot_start[None, :] <= positions) & (positions < slot_stop[None, :]) & (within < slot_length)[None, :]
        grouped = lax.dynamic_index_in_dim(query_blocks, owner, 0, keepdims=False).astype(jnp.float32)
        scores = jnp.einsum('tgrd,kgd->grtk', grouped, paired[:, :, :HD].astype(jnp.float32)) * score_scale
        weights, present = normalize(scores, allowed[None, None])
        context = jnp.einsum('grtk,kgd->tgrd', weights.astype(jnp.float32), paired[:, :, HD:].astype(jnp.float32))
        return (gate_value * context * present[0, 0][:, :, None, None]).astype(jnp.bfloat16)
    cross_blocks = lax.map(one_block, jnp.arange(NIMG, dtype=jnp.int32))
    cross_context = cross_blocks.reshape(TOKENS, H * HD)
    return (self_context, cross_context)
```

```python
import functools
import math

import jax
import jax.numpy as jnp
from jax import lax
from jax.experimental import pallas as pl
from jax.experimental.pallas import tpu as pltpu
from jax.sharding import PartitionSpec as P

LOW_SCORE = -1e30
LOG2E = 1.4426950408889634
NT = (((1,), (1,)), ((), ()))
NN = (((1,), (0,)), ((), ()))


def self_kernel(
    steps,
    head_rows,
    cached_rows,
    place_ref,
    own_ref,
    *refs,
):
    pieces = refs[: len(steps)]
    out_ref, keys, values, peak, total = refs[len(steps) :]
    parts = own_ref.shape[0]
    width = own_ref.shape[2]
    rows = head_rows
    heads = out_ref.shape[2] // width
    ring = len(steps) + 1
    here = place_ref[0]
    cached = cached_rows * parts * ring
    stretch = rows * ring
    scale = LOG2E / math.sqrt(width)

    ones = jnp.ones((rows, width), jnp.bfloat16)
    for start in range(0, cached + parts * stretch, rows):
        values[pl.ds(start, rows), width:] = ones

    def place(ref, base, owner):
        for part in range(parts):
            spot = pl.multiple_of(cached + part * stretch + owner * rows, rows)
            keys[pl.ds(spot, rows), :] = ref[part, base : base + rows, :]
            values[pl.ds(spot, rows), :width] = ref[part, base + rows : base + 2 * rows, :]
        tails = [
            ref[part, base + 2 * rows : base + 2 * rows + 2 * cached_rows, :].astype(jnp.float32)
            for part in range(parts)
        ]
        count = cached_rows * parts
        spot = pl.multiple_of(owner * count, count)
        keys[pl.ds(spot, count), :] = jnp.concatenate(
            [tail[:cached_rows] for tail in tails], 0
        ).astype(jnp.bfloat16)
        values[pl.ds(spot, count), :width] = jnp.concatenate(
            [tail[cached_rows:] for tail in tails], 0
        ).astype(jnp.bfloat16)

    place(own_ref, heads * rows, here)
    for step, ref in zip(steps, pieces):
        place(ref, 0, lax.rem(here + step + ring, ring))

    def fold(part, start, count, mask, first=False):
        block_keys = keys[pl.ds(start, count), :]
        block_values = values[pl.ds(start, count), :]
        for head in range(heads):
            query = own_ref[part, head * rows : (head + 1) * rows, :]
            scores = lax.dot_general(query, block_keys, NT, preferred_element_type=jnp.float32)
            if mask is not None:
                scores = jnp.where(mask, scores, LOW_SCORE)
            highest = jnp.max(scores, axis=1, keepdims=True)
            if first:
                top = jnp.broadcast_to(highest, (rows, width))
            else:
                top = jnp.maximum(peak[head], highest)
            weights = jnp.exp2((scores - top[:, :1]) * scale)
            added = lax.dot_general(
                weights.astype(jnp.bfloat16), block_values, NN, preferred_element_type=jnp.float32
            )
            if first:
                total[head] = added
            else:
                fade = jnp.exp2((peak[head] - top) * scale)
                total[head] = total[head] * jnp.concatenate([fade, fade], 1) + added
            peak[head] = top

    for part in range(parts):
        fold(part, 0, cached, None, first=True)
        for chunk in range(part):
            fold(part, cached + chunk * stretch, stretch, None)
        base = cached + part * stretch
        pair = 2 * rows

        def step_body(index, carry):
            fold(part, pl.multiple_of(base + index * pair, rows), pair, None)
            return carry

        lax.fori_loop(0, here // 2, step_body, 0)
        last = (here // 2) * pair
        offset = here * rows - last
        column = lax.broadcasted_iota(jnp.int32, (rows, pair), 1)
        line = lax.broadcasted_iota(jnp.int32, (rows, pair), 0)
        fold(part, pl.multiple_of(base + last, rows), pair, column <= line + offset)
        for head in range(heads):
            result = total[head]
            out_ref[part, :, head * width : (head + 1) * width] = (
                result[:, :width] / result[:, width:]
            ).astype(jnp.bfloat16)


def cross_kernel(
    slots,
    span_ref,
    gate_ref,
    query_ref,
    before_ref,
    own_ref,
    out_ref,
):
    rows = query_ref.shape[0]
    width = query_ref.shape[1]
    kv_width = own_ref.shape[1]
    head_dim = 128
    kv_heads = kv_width // (2 * head_dim)
    group = width // head_dim // kv_heads
    gate = gate_ref[0]
    column = lax.broadcasted_iota(jnp.int32, (rows, 2 * slots), 1)
    line = lax.broadcasted_iota(jnp.int32, (rows, 2 * slots), 0) + span_ref[0]
    late = column >= slots
    start = jnp.where(late, span_ref[4], span_ref[1])
    stop = jnp.where(late, span_ref[5], span_ref[2])
    length = jnp.where(late, span_ref[6] + slots, span_ref[3])
    allowed = (start <= line) & (line < stop) & (column < length)
    scale = 1.0 / math.sqrt(head_dim)
    for kv_head in range(kv_heads):
        base = kv_head * 2 * head_dim
        image_keys = jnp.concatenate(
            [before_ref[:, base : base + head_dim], own_ref[:, base : base + head_dim]], 0
        )
        image_values = jnp.concatenate(
            [
                before_ref[:, base + head_dim : base + 2 * head_dim],
                own_ref[:, base + head_dim : base + 2 * head_dim],
            ],
            0,
        )
        for member in range(group):
            spot = (kv_head * group + member) * head_dim
            query = query_ref[:, spot : spot + head_dim]
            scores = lax.dot_general(query, image_keys, NT, preferred_element_type=jnp.float32)
            scores = jnp.where(allowed, scores * scale, LOW_SCORE)
            highest = jnp.max(scores, axis=1, keepdims=True)
            weights = jnp.where(allowed, jnp.exp(scores - highest), 0.0)
            sums = jnp.sum(weights, axis=1, keepdims=True)
            sums = jnp.where(sums > 0.0, sums, 1.0)
            context = lax.dot_general(
                (weights / sums).astype(jnp.bfloat16),
                image_values,
                NN,
                preferred_element_type=jnp.float32,
            )
            out_ref[:, spot : spot + head_dim] = (gate * context).astype(jnp.bfloat16)


def shards(
    text_query,
    stretch_kv,
    cache_kv,
    cross_query,
    image_kv,
    image_start,
    image_stop,
    image_lengths,
    cross_gate,
):
    devices = lax.axis_size("seq")
    me = lax.axis_index("seq")
    rows, query_width = text_query.shape
    kv_heads = stretch_kv.shape[1]
    head_dim = stretch_kv.shape[2] // 2
    group = query_width // head_dim // kv_heads
    ring = devices // kv_heads
    cached_rows = cache_kv.shape[0]
    slots = image_kv.shape[1]
    columns = [[part * ring + spot for part in range(kv_heads)] for spot in range(ring)]

    def shift(values, step):
        pairs = [
            (part * ring + spot, part * ring + (spot + step) % ring)
            for part in range(kv_heads)
            for spot in range(ring)
        ]
        return lax.ppermute(values, "seq", pairs)

    query = jnp.transpose(
        text_query.reshape(rows, kv_heads, group, head_dim), (1, 2, 0, 3)
    ).reshape(kv_heads, group * rows, head_dim)

    def halves(values):
        swapped = jnp.transpose(values, (1, 0, 2))
        return [swapped[:, :, :head_dim], swapped[:, :, head_dim:]]

    message = jnp.concatenate([query] + halves(stretch_kv) + halves(cache_kv), 1)
    arrived = lax.all_to_all(
        message, "seq", split_axis=0, concat_axis=0, axis_index_groups=columns, tiled=True
    )

    own_image = image_kv.reshape(slots, kv_heads * 2 * head_dim)
    image_before = lax.ppermute(own_image, "seq", [(i, i + 1) for i in range(devices - 1)])

    block = arrived[:, group * rows :, :]
    up, down = block, block
    pieces, steps = [], []
    for step in range(1, ring // 2):
        up, down = shift(up, 1), shift(down, -1)
        pieces += [up, down]
        steps += [-step, step]
    half = kv_heads // 2
    far_up, far_down = shift(up[:half], 1), shift(down[half:], -1)
    pieces.append(jnp.concatenate([far_up, far_down], 0))
    steps.append(ring // 2)

    total_keys = kv_heads * ring * (rows + cached_rows)
    vmem = pl.BlockSpec(memory_space=pltpu.VMEM)
    smem = pl.BlockSpec(memory_space=pltpu.SMEM)
    self_heads = pl.pallas_call(
        functools.partial(self_kernel, tuple(steps), rows, cached_rows),
        out_shape=jax.ShapeDtypeStruct((kv_heads, rows, group * head_dim), jnp.bfloat16),
        in_specs=[smem] + [vmem] * (1 + len(pieces)),
        out_specs=vmem,
        scratch_shapes=[
            pltpu.VMEM((total_keys, head_dim), jnp.bfloat16),
            pltpu.VMEM((total_keys, 2 * head_dim), jnp.bfloat16),
            pltpu.VMEM((group, rows, head_dim), jnp.float32),
            pltpu.VMEM((group, rows, 2 * head_dim), jnp.float32),
        ],
        compiler_params=pltpu.CompilerParams(vmem_limit_bytes=48 * 2**20),
        name="self_attention",
    )((me % ring).reshape(1), arrived, *pieces)

    before = jnp.maximum(me - 1, 0)
    spans = jnp.stack(
        [
            me * rows,
            image_start[before],
            jnp.where(me > 0, image_stop[before], 0),
            image_lengths[before],
            image_start[me],
            image_stop[me],
            image_lengths[me],
        ]
    ).astype(jnp.int32)
    cross_context = pl.pallas_call(
        functools.partial(cross_kernel, slots),
        out_shape=jax.ShapeDtypeStruct(cross_query.shape, jnp.bfloat16),
        in_specs=[smem, smem, vmem, vmem, vmem],
        out_specs=vmem,
        compiler_params=pltpu.CompilerParams(vmem_limit_bytes=16 * 2**20),
        cost_estimate=pl.CostEstimate(
            flops=40_000_000, bytes_accessed=1_200_000, transcendentals=200_000
        ),
        name="cross_attention",
    )(spans, jnp.tanh(cross_gate), cross_query, image_before, own_image)

    returned = lax.all_to_all(
        self_heads, "seq", split_axis=0, concat_axis=0, axis_index_groups=columns, tiled=True
    )
    self_context = jnp.transpose(returned, (1, 0, 2)).reshape(rows, query_width)
    return (self_context, cross_context)


def solution(mesh):
    in_specs = (
        P(("doc", "seq"), None),
        P(("doc", "seq"), None, None),
        P(("doc", "seq"), None, None),
        P(("doc", "seq"), None),
        P(("doc", "seq"), None, None, None),
        P("doc"),
        P("doc"),
        P("doc"),
        P("doc"),
    )
    out_specs = (P(("doc", "seq"), None), P(("doc", "seq"), None))
    return jax.shard_map(shards, mesh=mesh, in_specs=in_specs, out_specs=out_specs, check_vma=False)
```

```python
import functools
import math

import jax
import jax.numpy as jnp
from jax import lax
from jax.experimental import pallas as pl
from jax.experimental.pallas import tpu as pltpu
from jax.sharding import PartitionSpec as P

LOW_SCORE = -1e30
LOG2E = 1.4426950408889634
MOST_TILES = 8
NT = (((1,), (1,)), ((), ()))
NN = (((1,), (0,)), ((), ()))


def pack_kernel(query_ref, stretch_ref, cache_ref, out_ref):
    rows = query_ref.shape[0]
    parts, _, width = out_ref.shape
    heads = query_ref.shape[1] // width // parts
    for part in range(parts):
        for head in range(heads):
            spot = (part * heads + head) * width
            out_ref[part, head * rows : (head + 1) * rows, :] = query_ref[:, spot : spot + width]
        base = heads * rows
        both = stretch_ref[:, part, :]
        out_ref[part, base : base + rows, :] = both[:, :width]
        out_ref[part, base + rows : base + 2 * rows, :] = both[:, width:]
        both = cache_ref[:, part, :].astype(jnp.float32)
        out_ref[part, base + 2 * rows :, :] = jnp.concatenate(
            [both[:, :width], both[:, width:]], 0
        ).astype(jnp.bfloat16)


def split(low, high):
    tiles = (high - low) // 128
    count = -(-tiles // MOST_TILES)
    edges = [low + 128 * (tiles * number // count) for number in range(count)] + [high]
    return list(zip(edges[:-1], edges[1:]))


def self_kernel(
    steps,
    counts,
    rows,
    ring,
    cached_rows,
    first,
    last,
    hold,
    caches,
    me_ref,
    own_ref,
    *refs,
):
    parts, _, width = own_ref.shape
    tail = 2 * cached_rows
    lines = own_ref.shape[1] - 2 * rows - tail
    heads = lines // rows
    here = lax.rem(me_ref[0], ring)
    scale = LOG2E / math.sqrt(width)
    refs = list(refs)

    def take(count):
        taken = refs[:count]
        del refs[:count]
        return taken

    pieces = [take(count) for count in counts]
    carried_caches = take(caches)
    carried = [] if first else take(3)
    if last:
        (out_ref,) = take(1)
    else:
        out_total, out_peak, out_sums = take(3)
    if hold:
        (out_cache,) = take(1)
    keys, values = refs

    sources = []
    for piece in pieces:
        if piece:
            sources.append([(ref, index, 0) for ref in piece for index in range(ref.shape[0])])
        else:
            sources.append([(own_ref, index, lines) for index in range(parts)])

    count = cached_rows * parts
    present = 0 if hold else count * len(steps) + sum(ref.shape[1] for ref in carried_caches)
    cached = -(-present // rows) * rows
    stretch = rows * len(steps)
    ones = jnp.ones((rows, width), jnp.bfloat16)
    for start in range(0, cached + parts * stretch, rows):
        values[start : start + rows, width:] = ones
    found = []
    for number, source in enumerate(sources):
        tails = []
        for part, (ref, index, base) in enumerate(source):
            place = cached + part * stretch + number * rows
            keys[place : place + rows, :] = ref[index, base : base + rows, :]
            values[place : place + rows, :width] = ref[index, base + rows : base + 2 * rows, :]
            tails.append(ref[index, base + 2 * rows : base + 2 * rows + tail, :].astype(jnp.float32))
        found.append(
            [
                jnp.concatenate([both[:cached_rows] for both in tails], 0).astype(jnp.bfloat16),
                jnp.concatenate([both[cached_rows:] for both in tails], 0).astype(jnp.bfloat16),
            ]
        )
    if hold:
        for number, pair in enumerate(found):
            for side in range(2):
                out_cache[side, number * count : (number + 1) * count, :] = pair[side]
    else:
        found += [(ref[0], ref[1]) for ref in carried_caches]
        place = 0
        for cache_keys, cache_values in found:
            size = cache_keys.shape[0]
            keys[place : place + size, :] = cache_keys
            values[place : place + size, :width] = cache_values
            place += size
        if place < cached:
            blank = jnp.zeros((cached - place, width), jnp.bfloat16)
            keys[place:cached, :] = blank
            values[place:cached, :width] = blank
    lane = lax.broadcasted_iota(jnp.int32, (1, rows), 1)
    edge = jnp.where(lane < present - (cached - rows), 0.0, LOW_SCORE)

    shifts = []
    for step in steps:
        if step == 0:
            line = lax.broadcasted_iota(jnp.int32, (lines, rows), 0) % rows
            column = lax.broadcasted_iota(jnp.int32, (lines, rows), 1)
            shifts.append(jnp.where(column <= line, 0.0, LOW_SCORE))
        else:
            owner = lax.rem(here + step + ring, ring)
            shifts.append(jnp.where(owner < here, 0.0, LOW_SCORE))

    for part in range(parts):
        query = own_ref[part, :lines, :]
        peak, total = None, None
        if not first:
            total = jnp.concatenate([carried[0][part], carried[2][part]], 1)
            peak = carried[1][part]
        full = cached + part * stretch
        chunks = split(0, full + stretch)
        if first:
            chunks = chunks[::-1]
        for low, high in chunks:
            scores = lax.dot_general(
                query, keys[low:high, :], NT, preferred_element_type=jnp.float32
            )
            tiles = []
            for spot in range(low, high, rows):
                tile = scores[:, spot - low : spot - low + rows] * scale
                if spot >= full:
                    tile = tile + shifts[(spot - full) // rows]
                elif spot == cached - rows and present < cached:
                    tile = tile + edge
                tiles.append(tile)
            top = jnp.max(functools.reduce(jnp.maximum, tiles), axis=1, keepdims=True)
            top = jnp.broadcast_to(top, (lines, width))
            if peak is not None:
                top = jnp.maximum(peak, top)
            weights = jnp.concatenate([jnp.exp2(tile - top) for tile in tiles], 1)
            added = lax.dot_general(
                weights.astype(jnp.bfloat16),
                values[low:high, :],
                NN,
                preferred_element_type=jnp.float32,
            )
            if peak is None:
                total = added
            else:
                fade = jnp.exp2(peak - top)
                total = total * jnp.concatenate([fade, fade], 1) + added
            peak = top
        if last:
            result = (total[:, :width] / total[:, width:]).astype(jnp.bfloat16)
            for head in range(heads):
                out_ref[part, :, head * width : (head + 1) * width] = result[
                    head * rows : (head + 1) * rows
                ]
        else:
            out_total[part] = total[:, :width]
            out_sums[part] = total[:, width:]
            out_peak[part] = peak


def cross_kernel(
    slots,
    me_ref,
    start_ref,
    stop_ref,
    length_ref,
    gate_ref,
    query_ref,
    before_ref,
    own_ref,
    out_ref,
):
    rows = query_ref.shape[0]
    width = query_ref.shape[1]
    kv_heads = own_ref.shape[1]
    head_dim = own_ref.shape[2] // 2
    group = width // head_dim // kv_heads
    me = me_ref[0]
    before = jnp.maximum(me - 1, 0)
    before_stop = jnp.where(me > 0, stop_ref[before], 0)
    gate = jnp.tanh(jnp.full((rows, head_dim), gate_ref[0], jnp.float32))
    column = lax.broadcasted_iota(jnp.int32, (rows, 2 * slots), 1)
    line = lax.broadcasted_iota(jnp.int32, (rows, 2 * slots), 0) + me * rows
    late = column >= slots
    start = jnp.where(late, start_ref[me], start_ref[before])
    stop = jnp.where(late, stop_ref[me], before_stop)
    length = jnp.where(late, length_ref[me] + slots, length_ref[before])
    allowed = (start <= line) & (line < stop) & (column < length)
    scale = 1.0 / math.sqrt(head_dim)
    for kv_head in range(kv_heads):
        image = jnp.concatenate([before_ref[:, kv_head, :], own_ref[:, kv_head, :]], 0)
        image_keys = image[:, :head_dim]
        image_values = image[:, head_dim:]
        for member in range(group):
            spot = (kv_head * group + member) * head_dim
            query = query_ref[:, spot : spot + head_dim]
            scores = lax.dot_general(query, image_keys, NT, preferred_element_type=jnp.float32)
            scores = jnp.where(allowed, scores * scale, LOW_SCORE)
            highest = jnp.max(scores, axis=1, keepdims=True)
            weights = jnp.where(allowed, jnp.exp(scores - highest), 0.0)
            sums = jnp.sum(weights, axis=1, keepdims=True)
            sums = jnp.where(sums > 0.0, sums, 1.0)
            context = lax.dot_general(
                (weights / sums).astype(jnp.bfloat16),
                image_values,
                NN,
                preferred_element_type=jnp.float32,
            )
            out_ref[:, spot : spot + head_dim] = (gate * context).astype(jnp.bfloat16)


def shards(
    text_query,
    stretch_kv,
    cache_kv,
    cross_query,
    image_kv,
    image_start,
    image_stop,
    image_lengths,
    cross_gate,
):
    devices = lax.axis_size("seq")
    me = lax.axis_index("seq")
    rows, query_width = text_query.shape
    kv_heads = stretch_kv.shape[1]
    head_dim = stretch_kv.shape[2] // 2
    group = query_width // head_dim // kv_heads
    ring = devices // kv_heads
    cached_rows = cache_kv.shape[0]
    slots = image_kv.shape[1]
    columns = [[part * ring + spot for part in range(kv_heads)] for spot in range(ring)]

    def shift(values, step):
        pairs = [
            (part * ring + spot, part * ring + (spot + step) % ring)
            for part in range(kv_heads)
            for spot in range(ring)
        ]
        return lax.ppermute(values, "seq", pairs)

    vmem = pl.BlockSpec(memory_space=pltpu.VMEM)
    smem = pl.BlockSpec(memory_space=pltpu.SMEM)
    lines = group * rows
    message = pl.pallas_call(
        pack_kernel,
        out_shape=jax.ShapeDtypeStruct(
            (kv_heads, lines + 2 * rows + 2 * cached_rows, head_dim), jnp.bfloat16
        ),
        in_specs=[vmem] * 3,
        out_specs=vmem,
        name="pack_message",
    )(text_query, stretch_kv, cache_kv)
    me_array = me.reshape(1).astype(jnp.int32)
    own_image = image_kv.reshape(image_kv.shape[1:])
    message, own_image = lax.optimization_barrier((message, own_image))
    image_before = lax.ppermute(own_image, "seq", [(i, i + 1) for i in range(devices - 1)])
    cross_context = pl.pallas_call(
        functools.partial(cross_kernel, slots),
        out_shape=jax.ShapeDtypeStruct(cross_query.shape, jnp.bfloat16),
        in_specs=[smem] * 5 + [vmem] * 3,
        out_specs=vmem,
        compiler_params=pltpu.CompilerParams(vmem_limit_bytes=16 * 2**20),
        cost_estimate=pl.CostEstimate(
            flops=400_000_000, bytes_accessed=1_200_000, transcendentals=200_000
        ),
        name="cross_attention",
    )(
        me_array,
        image_start,
        image_stop,
        image_lengths,
        cross_gate,
        cross_query,
        image_before,
        own_image,
    )

    arrived = lax.all_to_all(
        message, "seq", split_axis=0, concat_axis=0, axis_index_groups=columns, tiled=True
    )
    arrived, cross_context = lax.optimization_barrier((arrived, cross_context))

    def attend(steps, first, last, hold, caches, carried):
        pieces = [piece for step in steps for piece in arrivals[step]]
        count = kv_heads * cached_rows
        held = sum(cache.shape[1] for cache in caches) // count
        total_keys = kv_heads * len(steps) * rows
        if not hold:
            total_keys += -(-count * (len(steps) + held) // rows) * rows
        if last:
            out_shape = [jax.ShapeDtypeStruct((kv_heads, rows, group * head_dim), jnp.bfloat16)]
        else:
            out_shape = [jax.ShapeDtypeStruct((kv_heads, lines, head_dim), jnp.float32)] * 3
        if hold:
            out_shape.append(
                jax.ShapeDtypeStruct((2, count * len(steps), head_dim), jnp.bfloat16)
            )
        work = kv_heads * lines * len(steps) * rows * 3
        return pl.pallas_call(
            functools.partial(
                self_kernel,
                steps,
                tuple(len(arrivals[step]) for step in steps),
                rows,
                ring,
                cached_rows,
                first,
                last,
                hold,
                len(caches),
            ),
            out_shape=out_shape,
            in_specs=[smem] + [vmem] * (1 + len(pieces) + len(caches) + len(carried)),
            out_specs=[vmem] * len(out_shape),
            scratch_shapes=[
                pltpu.VMEM((total_keys, head_dim), jnp.bfloat16),
                pltpu.VMEM((total_keys, 2 * head_dim), jnp.bfloat16),
            ],
            compiler_params=pltpu.CompilerParams(vmem_limit_bytes=32 * 2**20),
            cost_estimate=pl.CostEstimate(
                flops=4 * work * head_dim, bytes_accessed=2_000_000, transcendentals=work
            ),
            name="self_attention",
        )(me_array, arrived, *pieces, *caches, *carried)

    up = down = arrived[:, lines:, :]
    arrivals = {0: ()}
    state, caches = (), ()
    steps = (0,)
    for step in range(1, ring // 2):
        up, down = shift(up, 1), shift(down, -1)
        *state, cache = attend(steps, step == 1, False, True, (), state)
        caches += (cache,)
        up, state = lax.optimization_barrier((up, state))
        arrivals[-step], arrivals[step] = (up,), (down,)
        steps = (-step, step)
    arrivals[ring // 2] = (shift(up, 1),)
    state = attend(steps, False, False, False, caches, state)
    (self_heads,) = attend((ring // 2,), False, True, False, (), state)

    returned = lax.all_to_all(
        self_heads, "seq", split_axis=0, concat_axis=0, axis_index_groups=columns, tiled=True
    )
    self_context = jnp.concatenate([returned[part] for part in range(kv_heads)], 1)
    return (self_context, cross_context)


def solution(mesh):
    in_specs = (
        P(("doc", "seq"), None),
        P(("doc", "seq"), None, None),
        P(("doc", "seq"), None, None),
        P(("doc", "seq"), None),
        P(("doc", "seq"), None, None, None),
        P("doc"),
        P("doc"),
        P("doc"),
        P("doc"),
    )
    out_specs = (P(("doc", "seq"), None), P(("doc", "seq"), None))
    return jax.shard_map(shards, mesh=mesh, in_specs=in_specs, out_specs=out_specs, check_vma=False)
```

```python
import functools
import math

import jax
import jax.numpy as jnp
from jax import lax
from jax.experimental import pallas as pl
from jax.experimental.pallas import tpu as pltpu
from jax.sharding import PartitionSpec as P

LOW_SCORE = -1e30
LOG2E = 1.4426950408889634
MOST_TILES = 8
NT = (((1,), (1,)), ((), ()))
NN = (((1,), (0,)), ((), ()))


def pack_kernel(query_ref, stretch_ref, cache_ref, out_ref):
    rows = query_ref.shape[0]
    parts, _, width = out_ref.shape
    heads = query_ref.shape[1] // width // parts
    for part in range(parts):
        for head in range(heads):
            spot = (part * heads + head) * width
            out_ref[part, head * rows : (head + 1) * rows, :] = query_ref[:, spot : spot + width]
    base = heads * rows
    stretch = jnp.swapaxes(stretch_ref[...], 0, 1)
    out_ref[:, base : base + rows, :] = stretch[:, :, :width]
    out_ref[:, base + rows : base + 2 * rows, :] = stretch[:, :, width:]
    cache = jnp.swapaxes(cache_ref[...].astype(jnp.float32), 0, 1)
    out_ref[:, base + 2 * rows :, :] = jnp.concatenate(
        [cache[:, :, :width], cache[:, :, width:]], 1
    ).astype(jnp.bfloat16)


def split(low, high):
    tiles = (high - low) // 128
    count = -(-tiles // MOST_TILES)
    edges = [low + 128 * (tiles * number // count) for number in range(count)] + [high]
    return list(zip(edges[:-1], edges[1:]))


def self_kernel(
    steps,
    counts,
    rows,
    ring,
    cached_rows,
    first,
    last,
    hold,
    caches,
    me_ref,
    own_ref,
    *refs,
):
    parts, _, width = own_ref.shape
    tail = 2 * cached_rows
    lines = own_ref.shape[1] - 2 * rows - tail
    heads = lines // rows
    here = lax.rem(me_ref[0], ring)
    scale = LOG2E / math.sqrt(width)
    refs = list(refs)

    def take(count):
        taken = refs[:count]
        del refs[:count]
        return taken

    pieces = [take(count) for count in counts]
    carried_caches = take(caches)
    carried = [] if first else take(3)
    if last:
        (out_ref,) = take(1)
    else:
        out_total, out_peak, out_sums = take(3)
    if hold:
        (out_cache,) = take(1)
    keys, values = refs

    sources = []
    for piece in pieces:
        if piece:
            sources.append([(ref, index, 0) for ref in piece for index in range(ref.shape[0])])
        else:
            sources.append([(own_ref, index, lines) for index in range(parts)])

    count = cached_rows * parts
    present = 0 if hold else count * len(steps) + sum(ref.shape[1] for ref in carried_caches)
    cached = -(-present // rows) * rows
    stretch = rows * len(steps)
    ones = jnp.ones((rows, width), jnp.bfloat16)
    for start in range(0, cached + parts * stretch, rows):
        values[start : start + rows, width:] = ones
    found = []
    for number, source in enumerate(sources):
        tails = []
        for part, (ref, index, base) in enumerate(source):
            place = cached + part * stretch + number * rows
            keys[place : place + rows, :] = ref[index, base : base + rows, :]
            values[place : place + rows, :width] = ref[index, base + rows : base + 2 * rows, :]
            tails.append(ref[index, base + 2 * rows : base + 2 * rows + tail, :].astype(jnp.float32))
        found.append(
            [
                jnp.concatenate([both[:cached_rows] for both in tails], 0).astype(jnp.bfloat16),
                jnp.concatenate([both[cached_rows:] for both in tails], 0).astype(jnp.bfloat16),
            ]
        )
    if hold:
        for number, pair in enumerate(found):
            for side in range(2):
                out_cache[side, number * count : (number + 1) * count, :] = pair[side]
    else:
        found += [(ref[0], ref[1]) for ref in carried_caches]
        place = 0
        for cache_keys, cache_values in found:
            size = cache_keys.shape[0]
            keys[place : place + size, :] = cache_keys
            values[place : place + size, :width] = cache_values
            place += size
        if place < cached:
            blank = jnp.zeros((cached - place, width), jnp.bfloat16)
            keys[place:cached, :] = blank
            values[place:cached, :width] = blank
    lane = lax.broadcasted_iota(jnp.int32, (1, rows), 1)
    edge = jnp.where(lane < present - (cached - rows), 0.0, LOW_SCORE)

    def fold(part, valid):
        query = own_ref[part, :lines, :]
        peak, total = None, None
        if not first:
            total = jnp.concatenate([carried[0][part], carried[2][part]], 1)
            peak = carried[1][part]
        full = cached + part * stretch
        chunks = split(0, full + valid * rows)
        if first:
            chunks = chunks[::-1]
        for low, high in chunks:
            scores = lax.dot_general(
                query, keys[low:high, :], NT, preferred_element_type=jnp.float32
            )
            tiles = []
            for spot in range(low, high, rows):
                tile = scores[:, spot - low : spot - low + rows] * scale
                if spot >= full and steps[(spot - full) // rows] == 0:
                    line = lax.broadcasted_iota(jnp.int32, (lines, rows), 0) % rows
                    column = lax.broadcasted_iota(jnp.int32, (lines, rows), 1)
                    tile = jnp.where(column <= line, tile, LOW_SCORE)
                elif spot == cached - rows and present < cached:
                    tile = tile + edge
                tiles.append(tile)
            top = jnp.max(functools.reduce(jnp.maximum, tiles), axis=1, keepdims=True)
            top = jnp.broadcast_to(top, (lines, width))
            if peak is not None:
                top = jnp.maximum(peak, top)
            weights = jnp.concatenate([jnp.exp2(tile - top) for tile in tiles], 1)
            added = lax.dot_general(
                weights.astype(jnp.bfloat16),
                values[low:high, :],
                NN,
                preferred_element_type=jnp.float32,
            )
            if peak is None:
                total = added
            else:
                fade = jnp.exp2(peak - top)
                total = total * jnp.concatenate([fade, fade], 1) + added
            peak = top
        if last:
            result = (total[:, :width] / total[:, width:]).astype(jnp.bfloat16)
            for head in range(heads):
                out_ref[part, :, head * width : (head + 1) * width] = result[
                    head * rows : (head + 1) * rows
                ]
        else:
            out_total[part] = total[:, :width]
            out_sums[part] = total[:, width:]
            out_peak[part] = peak

    if steps == (0,):
        for part in range(parts):
            fold(part, 1)
        return
    owners = [lax.rem(here + step + ring, ring) for step in steps]
    earlier = sum((owner < here).astype(jnp.int32) for owner in owners)
    for valid in range(len(steps) + 1):

        @pl.when(earlier == valid)
        def _():
            for part in range(parts):
                fold(part, valid)


def cross_kernel(
    slots,
    me_ref,
    start_ref,
    stop_ref,
    length_ref,
    gate_ref,
    query_ref,
    before_ref,
    own_ref,
    out_ref,
):
    rows = query_ref.shape[0]
    width = query_ref.shape[1]
    kv_heads = own_ref.shape[1]
    head_dim = own_ref.shape[2] // 2
    group = width // head_dim // kv_heads
    me = me_ref[0]
    before = jnp.maximum(me - 1, 0)
    before_stop = jnp.where(me > 0, stop_ref[before], 0)
    gate = jnp.tanh(jnp.full((rows, head_dim), gate_ref[0], jnp.float32))
    column = lax.broadcasted_iota(jnp.int32, (rows, 2 * slots), 1)
    line = lax.broadcasted_iota(jnp.int32, (rows, 2 * slots), 0) + me * rows
    late = column >= slots
    start = jnp.where(late, start_ref[me], start_ref[before])
    stop = jnp.where(late, stop_ref[me], before_stop)
    length = jnp.where(late, length_ref[me] + slots, length_ref[before])
    allowed = (start <= line) & (line < stop) & (column < length)
    scale = 1.0 / math.sqrt(head_dim)
    for kv_head in range(kv_heads):
        image = jnp.concatenate([before_ref[:, kv_head, :], own_ref[:, kv_head, :]], 0)
        image_keys = image[:, :head_dim]
        image_values = image[:, head_dim:]
        for member in range(group):
            spot = (kv_head * group + member) * head_dim
            query = query_ref[:, spot : spot + head_dim]
            scores = lax.dot_general(query, image_keys, NT, preferred_element_type=jnp.float32)
            scores = jnp.where(allowed, scores * scale, LOW_SCORE)
            highest = jnp.max(scores, axis=1, keepdims=True)
            weights = jnp.where(allowed, jnp.exp(scores - highest), 0.0)
            sums = jnp.sum(weights, axis=1, keepdims=True)
            sums = jnp.where(sums > 0.0, sums, 1.0)
            context = lax.dot_general(
                (weights / sums).astype(jnp.bfloat16),
                image_values,
                NN,
                preferred_element_type=jnp.float32,
            )
            out_ref[:, spot : spot + head_dim] = (gate * context).astype(jnp.bfloat16)


def shards(
    text_query,
    stretch_kv,
    cache_kv,
    cross_query,
    image_kv,
    image_start,
    image_stop,
    image_lengths,
    cross_gate,
):
    devices = lax.axis_size("seq")
    me = lax.axis_index("seq")
    rows, query_width = text_query.shape
    kv_heads = stretch_kv.shape[1]
    head_dim = stretch_kv.shape[2] // 2
    group = query_width // head_dim // kv_heads
    ring = devices // kv_heads
    cached_rows = cache_kv.shape[0]
    slots = image_kv.shape[1]
    columns = [[part * ring + spot for part in range(kv_heads)] for spot in range(ring)]

    def shift(values, step):
        pairs = [
            (part * ring + spot, part * ring + (spot + step) % ring)
            for part in range(kv_heads)
            for spot in range(ring)
        ]
        return lax.ppermute(values, "seq", pairs)

    vmem = pl.BlockSpec(memory_space=pltpu.VMEM)
    smem = pl.BlockSpec(memory_space=pltpu.SMEM)
    lines = group * rows
    message = pl.pallas_call(
        pack_kernel,
        out_shape=jax.ShapeDtypeStruct(
            (kv_heads, lines + 2 * rows + 2 * cached_rows, head_dim), jnp.bfloat16
        ),
        in_specs=[vmem] * 3,
        out_specs=vmem,
        name="pack_message",
    )(text_query, stretch_kv, cache_kv)
    me_array = me.reshape(1).astype(jnp.int32)
    own_image = image_kv.reshape(image_kv.shape[1:])
    message, own_image = lax.optimization_barrier((message, own_image))
    image_before = lax.ppermute(own_image, "seq", [(i, i + 1) for i in range(devices - 1)])
    cross_context = pl.pallas_call(
        functools.partial(cross_kernel, slots),
        out_shape=jax.ShapeDtypeStruct(cross_query.shape, jnp.bfloat16),
        in_specs=[smem] * 5 + [vmem] * 3,
        out_specs=vmem,
        compiler_params=pltpu.CompilerParams(vmem_limit_bytes=16 * 2**20),
        cost_estimate=pl.CostEstimate(
            flops=400_000_000, bytes_accessed=1_200_000, transcendentals=200_000
        ),
        name="cross_attention",
    )(
        me_array,
        image_start,
        image_stop,
        image_lengths,
        cross_gate,
        cross_query,
        image_before,
        own_image,
    )

    arrived = lax.all_to_all(
        message, "seq", split_axis=0, concat_axis=0, axis_index_groups=columns, tiled=True
    )
    arrived, cross_context = lax.optimization_barrier((arrived, cross_context))

    def attend(steps, first, last, hold, caches, carried):
        pieces = [piece for step in steps for piece in arrivals[step]]
        count = kv_heads * cached_rows
        held = sum(cache.shape[1] for cache in caches) // count
        total_keys = kv_heads * len(steps) * rows
        if not hold:
            total_keys += -(-count * (len(steps) + held) // rows) * rows
        if last:
            out_shape = [jax.ShapeDtypeStruct((kv_heads, rows, group * head_dim), jnp.bfloat16)]
        else:
            out_shape = [jax.ShapeDtypeStruct((kv_heads, lines, head_dim), jnp.float32)] * 3
        if hold:
            out_shape.append(
                jax.ShapeDtypeStruct((2, count * len(steps), head_dim), jnp.bfloat16)
            )
        work = kv_heads * lines * len(steps) * rows * 3
        return pl.pallas_call(
            functools.partial(
                self_kernel,
                steps,
                tuple(len(arrivals[step]) for step in steps),
                rows,
                ring,
                cached_rows,
                first,
                last,
                hold,
                len(caches),
            ),
            out_shape=out_shape,
            in_specs=[smem] + [vmem] * (1 + len(pieces) + len(caches) + len(carried)),
            out_specs=[vmem] * len(out_shape),
            scratch_shapes=[
                pltpu.VMEM((total_keys, head_dim), jnp.bfloat16),
                pltpu.VMEM((total_keys, 2 * head_dim), jnp.bfloat16),
            ],
            compiler_params=pltpu.CompilerParams(vmem_limit_bytes=32 * 2**20),
            cost_estimate=pl.CostEstimate(
                flops=4 * work * head_dim, bytes_accessed=2_000_000, transcendentals=work
            ),
            name="self_attention",
        )(me_array, arrived, *pieces, *caches, *carried)

    up = down = arrived[:, lines:, :]
    arrivals = {0: ()}
    state, caches = (), ()
    steps = (0,)
    for step in range(1, ring // 2):
        down, up = shift(down, -1), shift(up, 1)
        *state, cache = attend(steps, step == 1, False, True, (), state)
        caches += (cache,)
        down, state = lax.optimization_barrier((down, state))
        arrivals[-step], arrivals[step] = (up,), (down,)
        steps = (-step, step)
    arrivals[ring // 2] = (shift(down, -1),)
    state = attend(steps, False, False, False, caches, state)
    (self_heads,) = attend((ring // 2,), False, True, False, (), state)

    returned = lax.all_to_all(
        self_heads, "seq", split_axis=0, concat_axis=0, axis_index_groups=columns, tiled=True
    )
    self_context = jnp.concatenate([returned[part] for part in range(kv_heads)], 1)
    return (self_context, cross_context)


def solution(mesh):
    in_specs = (
        P(("doc", "seq"), None),
        P(("doc", "seq"), None, None),
        P(("doc", "seq"), None, None),
        P(("doc", "seq"), None),
        P(("doc", "seq"), None, None, None),
        P("doc"),
        P("doc"),
        P("doc"),
        P("doc"),
    )
    out_specs = (P(("doc", "seq"), None), P(("doc", "seq"), None))
    return jax.shard_map(shards, mesh=mesh, in_specs=in_specs, out_specs=out_specs, check_vma=False)
```

```python
import functools
import math

import jax
import jax.numpy as jnp
from jax import lax
from jax.experimental import pallas as pl
from jax.experimental.pallas import tpu as pltpu
from jax.sharding import PartitionSpec as P

LOW_SCORE = -1e30
LOG2E = 1.4426950408889634
MOST_TILES = 8
NT = (((1,), (1,)), ((), ()))
NN = (((1,), (0,)), ((), ()))


def pack_kernel(query_ref, stretch_ref, cache_ref, out_ref):
    rows = query_ref.shape[0]
    parts, _, width = out_ref.shape
    heads = query_ref.shape[1] // width // parts
    for part in range(parts):
        for head in range(heads):
            spot = (part * heads + head) * width
            out_ref[part, head * rows : (head + 1) * rows, :] = query_ref[:, spot : spot + width]
    base = heads * rows
    stretch = jnp.swapaxes(stretch_ref[...], 0, 1)
    out_ref[:, base : base + rows, :] = stretch[:, :, :width]
    out_ref[:, base + rows : base + 2 * rows, :] = stretch[:, :, width:]
    cache = jnp.swapaxes(cache_ref[...].astype(jnp.float32), 0, 1)
    out_ref[:, base + 2 * rows :, :] = jnp.concatenate(
        [cache[:, :, :width], cache[:, :, width:]], 1
    ).astype(jnp.bfloat16)


def split(low, high):
    tiles = (high - low) // 128
    count = -(-tiles // MOST_TILES)
    edges = [low + 128 * (tiles * number // count) for number in range(count)] + [high]
    return list(zip(edges[:-1], edges[1:]))


def self_kernel(
    steps,
    counts,
    rows,
    ring,
    cached_rows,
    first,
    last,
    hold,
    caches,
    me_ref,
    own_ref,
    *refs,
):
    parts, _, width = own_ref.shape
    tail = 2 * cached_rows
    lines = own_ref.shape[1] - 2 * rows - tail
    heads = lines // rows
    here = lax.rem(me_ref[0], ring)
    scale = LOG2E / math.sqrt(width)
    refs = list(refs)

    def take(count):
        taken = refs[:count]
        del refs[:count]
        return taken

    pieces = [take(count) for count in counts]
    carried_caches = take(caches)
    carried = [] if first else take(3)
    if last:
        (out_ref,) = take(1)
    else:
        out_total, out_peak, out_sums = take(3)
    if hold:
        (out_cache,) = take(1)
    keys, values = refs

    sources = []
    for piece in pieces:
        if piece:
            sources.append([(ref, index, 0) for ref in piece for index in range(ref.shape[0])])
        else:
            sources.append([(own_ref, index, lines) for index in range(parts)])

    count = cached_rows * parts
    present = 0 if hold else count * len(steps) + sum(ref.shape[1] for ref in carried_caches)
    cached = -(-present // rows) * rows
    stretch = rows * len(steps)
    ones = jnp.ones((rows, width), jnp.bfloat16)
    for start in range(0, cached + parts * stretch, rows):
        values[start : start + rows, width:] = ones
    found = []
    for number, source in enumerate(sources):
        tails = []
        for part, (ref, index, base) in enumerate(source):
            place = cached + part * stretch + number * rows
            keys[place : place + rows, :] = ref[index, base : base + rows, :]
            values[place : place + rows, :width] = ref[index, base + rows : base + 2 * rows, :]
            tails.append(ref[index, base + 2 * rows : base + 2 * rows + tail, :].astype(jnp.float32))
        found.append(
            [
                jnp.concatenate([both[:cached_rows] for both in tails], 0).astype(jnp.bfloat16),
                jnp.concatenate([both[cached_rows:] for both in tails], 0).astype(jnp.bfloat16),
            ]
        )
    if hold:
        for number, pair in enumerate(found):
            for side in range(2):
                out_cache[side, number * count : (number + 1) * count, :] = pair[side]
    else:
        found += [(ref[0], ref[1]) for ref in carried_caches]
        place = 0
        for cache_keys, cache_values in found:
            size = cache_keys.shape[0]
            keys[place : place + size, :] = cache_keys
            values[place : place + size, :width] = cache_values
            place += size
        if place < cached:
            blank = jnp.zeros((cached - place, width), jnp.bfloat16)
            keys[place:cached, :] = blank
            values[place:cached, :width] = blank
    lane = lax.broadcasted_iota(jnp.int32, (1, rows), 1)
    edge = jnp.where(lane < present - (cached - rows), 0.0, LOW_SCORE)

    def fold(part, valid):
        query = own_ref[part, :lines, :]
        peak, total = None, None
        if not first:
            total = jnp.concatenate([carried[0][part], carried[2][part]], 1)
            peak = carried[1][part]
        full = cached + part * stretch
        chunks = split(0, full + valid * rows)
        if first:
            chunks = chunks[::-1]
        for low, high in chunks:
            scores = lax.dot_general(
                query, keys[low:high, :], NT, preferred_element_type=jnp.float32
            )
            tiles = []
            for spot in range(low, high, rows):
                tile = scores[:, spot - low : spot - low + rows] * scale
                if spot >= full and steps[(spot - full) // rows] == 0:
                    line = lax.broadcasted_iota(jnp.int32, (lines, rows), 0) % rows
                    column = lax.broadcasted_iota(jnp.int32, (lines, rows), 1)
                    tile = jnp.where(column <= line, tile, LOW_SCORE)
                elif spot == cached - rows and present < cached:
                    tile = tile + edge
                tiles.append(tile)
            top = jnp.max(functools.reduce(jnp.maximum, tiles), axis=1, keepdims=True)
            top = jnp.broadcast_to(top, (lines, width))
            if peak is not None:
                top = jnp.maximum(peak, top)
            weights = jnp.concatenate([jnp.exp2(tile - top) for tile in tiles], 1)
            added = lax.dot_general(
                weights.astype(jnp.bfloat16),
                values[low:high, :],
                NN,
                preferred_element_type=jnp.float32,
            )
            if peak is None:
                total = added
            else:
                fade = jnp.exp2(peak - top)
                total = total * jnp.concatenate([fade, fade], 1) + added
            peak = top
        if last:
            result = (total[:, :width] / total[:, width:]).astype(jnp.bfloat16)
            for head in range(heads):
                out_ref[part, :, head * width : (head + 1) * width] = result[
                    head * rows : (head + 1) * rows
                ]
        else:
            out_total[part] = total[:, :width]
            out_sums[part] = total[:, width:]
            out_peak[part] = peak

    if steps == (0,):
        for part in reversed(range(parts)):
            fold(part, 1)
        return
    owners = [lax.rem(here + step + ring, ring) for step in steps]
    earlier = sum((owner < here).astype(jnp.int32) for owner in owners)
    for valid in range(len(steps) + 1):

        @pl.when(earlier == valid)
        def _():
            for part in reversed(range(parts)):
                fold(part, valid)


def cross_kernel(
    slots,
    me_ref,
    start_ref,
    stop_ref,
    length_ref,
    gate_ref,
    query_ref,
    before_ref,
    own_ref,
    out_ref,
):
    rows = query_ref.shape[0]
    width = query_ref.shape[1]
    kv_heads = own_ref.shape[1]
    head_dim = own_ref.shape[2] // 2
    group = width // head_dim // kv_heads
    me = me_ref[0]
    before = jnp.maximum(me - 1, 0)
    before_stop = jnp.where(me > 0, stop_ref[before], 0)
    gate = jnp.tanh(jnp.full((rows, head_dim), gate_ref[0], jnp.float32))
    column = lax.broadcasted_iota(jnp.int32, (rows, 2 * slots), 1)
    line = lax.broadcasted_iota(jnp.int32, (rows, 2 * slots), 0) + me * rows
    late = column >= slots
    start = jnp.where(late, start_ref[me], start_ref[before])
    stop = jnp.where(late, stop_ref[me], before_stop)
    length = jnp.where(late, length_ref[me] + slots, length_ref[before])
    allowed = (start <= line) & (line < stop) & (column < length)
    scale = 1.0 / math.sqrt(head_dim)
    for kv_head in range(kv_heads):
        image = jnp.concatenate([before_ref[:, kv_head, :], own_ref[:, kv_head, :]], 0)
        image_keys = image[:, :head_dim]
        image_values = image[:, head_dim:]
        for member in range(group):
            spot = (kv_head * group + member) * head_dim
            query = query_ref[:, spot : spot + head_dim]
            scores = lax.dot_general(query, image_keys, NT, preferred_element_type=jnp.float32)
            scores = jnp.where(allowed, scores * scale, LOW_SCORE)
            highest = jnp.max(scores, axis=1, keepdims=True)
            weights = jnp.where(allowed, jnp.exp(scores - highest), 0.0)
            sums = jnp.sum(weights, axis=1, keepdims=True)
            sums = jnp.where(sums > 0.0, sums, 1.0)
            context = lax.dot_general(
                (weights / sums).astype(jnp.bfloat16),
                image_values,
                NN,
                preferred_element_type=jnp.float32,
            )
            out_ref[:, spot : spot + head_dim] = (gate * context).astype(jnp.bfloat16)


def shards(
    text_query,
    stretch_kv,
    cache_kv,
    cross_query,
    image_kv,
    image_start,
    image_stop,
    image_lengths,
    cross_gate,
):
    devices = lax.axis_size("seq")
    me = lax.axis_index("seq")
    rows, query_width = text_query.shape
    kv_heads = stretch_kv.shape[1]
    head_dim = stretch_kv.shape[2] // 2
    group = query_width // head_dim // kv_heads
    ring = devices // kv_heads
    cached_rows = cache_kv.shape[0]
    slots = image_kv.shape[1]
    columns = [[part * ring + spot for part in range(kv_heads)] for spot in range(ring)]

    def shift(values, step):
        pairs = [
            (part * ring + spot, part * ring + (spot + step) % ring)
            for part in range(kv_heads)
            for spot in range(ring)
        ]
        return lax.ppermute(values, "seq", pairs)

    vmem = pl.BlockSpec(memory_space=pltpu.VMEM)
    smem = pl.BlockSpec(memory_space=pltpu.SMEM)
    lines = group * rows
    message = pl.pallas_call(
        pack_kernel,
        out_shape=jax.ShapeDtypeStruct(
            (kv_heads, lines + 2 * rows + 2 * cached_rows, head_dim), jnp.bfloat16
        ),
        in_specs=[vmem] * 3,
        out_specs=vmem,
        name="pack_message",
    )(text_query, stretch_kv, cache_kv)
    me_array = me.reshape(1).astype(jnp.int32)
    own_image = image_kv.reshape(image_kv.shape[1:])
    message, own_image = lax.optimization_barrier((message, own_image))
    image_before = lax.ppermute(own_image, "seq", [(i, i + 1) for i in range(devices - 1)])
    cross_context = pl.pallas_call(
        functools.partial(cross_kernel, slots),
        out_shape=jax.ShapeDtypeStruct(cross_query.shape, jnp.bfloat16),
        in_specs=[smem] * 5 + [vmem] * 3,
        out_specs=vmem,
        compiler_params=pltpu.CompilerParams(vmem_limit_bytes=16 * 2**20),
        cost_estimate=pl.CostEstimate(
            flops=400_000_000, bytes_accessed=1_200_000, transcendentals=200_000
        ),
        name="cross_attention",
    )(
        me_array,
        image_start,
        image_stop,
        image_lengths,
        cross_gate,
        cross_query,
        image_before,
        own_image,
    )

    arrived = lax.all_to_all(
        message, "seq", split_axis=0, concat_axis=0, axis_index_groups=columns, tiled=True
    )
    arrived, cross_context = lax.optimization_barrier((arrived, cross_context))

    def attend(steps, first, last, hold, caches, carried):
        pieces = [piece for step in steps for piece in arrivals[step]]
        count = kv_heads * cached_rows
        held = sum(cache.shape[1] for cache in caches) // count
        total_keys = kv_heads * len(steps) * rows
        if not hold:
            total_keys += -(-count * (len(steps) + held) // rows) * rows
        if last:
            out_shape = [jax.ShapeDtypeStruct((kv_heads, rows, group * head_dim), jnp.bfloat16)]
        else:
            out_shape = [jax.ShapeDtypeStruct((kv_heads, lines, head_dim), jnp.float32)] * 3
        if hold:
            out_shape.append(
                jax.ShapeDtypeStruct((2, count * len(steps), head_dim), jnp.bfloat16)
            )
        work = kv_heads * lines * len(steps) * rows * 3
        return pl.pallas_call(
            functools.partial(
                self_kernel,
                steps,
                tuple(len(arrivals[step]) for step in steps),
                rows,
                ring,
                cached_rows,
                first,
                last,
                hold,
                len(caches),
            ),
            out_shape=out_shape,
            in_specs=[smem] + [vmem] * (1 + len(pieces) + len(caches) + len(carried)),
            out_specs=[vmem] * len(out_shape),
            scratch_shapes=[
                pltpu.VMEM((total_keys, head_dim), jnp.bfloat16),
                pltpu.VMEM((total_keys, 2 * head_dim), jnp.bfloat16),
            ],
            compiler_params=pltpu.CompilerParams(vmem_limit_bytes=32 * 2**20),
            cost_estimate=pl.CostEstimate(
                flops=4 * work * head_dim, bytes_accessed=2_000_000, transcendentals=work
            ),
            name="self_attention",
        )(me_array, arrived, *pieces, *caches, *carried)

    up = down = arrived[:, lines:, :]
    arrivals = {0: ()}
    state, caches = (), ()
    steps = (0,)
    for step in range(1, ring // 2):
        down, up = shift(down, -1), shift(up, 1)
        *state, cache = attend(steps, step == 1, False, True, (), state)
        caches += (cache,)
        down, state = lax.optimization_barrier((down, state))
        arrivals[-step], arrivals[step] = (up,), (down,)
        steps = (-step, step)
    arrivals[ring // 2] = (shift(down, -1),)
    state = attend(steps, False, False, False, caches, state)
    (self_heads,) = attend((ring // 2,), False, True, False, (), state)

    returned = lax.all_to_all(
        self_heads, "seq", split_axis=0, concat_axis=0, axis_index_groups=columns, tiled=True
    )
    self_context = jnp.concatenate([returned[part] for part in range(kv_heads)], 1)
    return (self_context, cross_context)


def solution(mesh):
    in_specs = (
        P(("doc", "seq"), None),
        P(("doc", "seq"), None, None),
        P(("doc", "seq"), None, None),
        P(("doc", "seq"), None),
        P(("doc", "seq"), None, None, None),
        P("doc"),
        P("doc"),
        P("doc"),
        P("doc"),
    )
    out_specs = (P(("doc", "seq"), None), P(("doc", "seq"), None))
    return jax.shard_map(shards, mesh=mesh, in_specs=in_specs, out_specs=out_specs, check_vma=False)
```

```python
import functools
import math

import jax
import jax.numpy as jnp
from jax import lax
from jax.experimental import pallas as pl
from jax.experimental.pallas import tpu as pltpu
from jax.sharding import PartitionSpec as P

LOW_SCORE = -1e30
LOG2E = 1.4426950408889634
MOST_TILES = 8
NT = (((1,), (1,)), ((), ()))
NN = (((1,), (0,)), ((), ()))


def pack_kernel(query_ref, stretch_ref, cache_ref, out_ref, blocks):
    rows = query_ref.shape[0]
    parts, lines, width = out_ref.shape
    heads = query_ref.shape[1] // width // parts
    base = heads * rows
    step = pl.program_id(0)

    @pl.when(step == 0)
    def _():
        stretch = jnp.swapaxes(stretch_ref[...], 0, 1)
        blocks[:, :rows, :] = stretch[:, :, :width]
        blocks[:, rows : 2 * rows, :] = stretch[:, :, width:]
        cache = jnp.swapaxes(cache_ref[...].astype(jnp.float32), 0, 1)
        blocks[:, 2 * rows :, :] = jnp.concatenate(
            [cache[:, :, :width], cache[:, :, width:]], 1
        ).astype(jnp.bfloat16)

    for part in range(parts):
        for head in range(heads):
            spot = (part * heads + head) * width
            out_ref[part, head * rows : (head + 1) * rows, :] = query_ref[:, spot : spot + width]
    out_ref[:, base:lines, :] = blocks[pl.ds(step * parts, parts), :, :]


def split(low, high):
    tiles = (high - low) // 128
    count = -(-tiles // MOST_TILES)
    edges = [low + 128 * (tiles * number // count) for number in range(count)] + [high]
    return list(zip(edges[:-1], edges[1:]))


def self_kernel(
    steps,
    counts,
    rows,
    ring,
    cached_rows,
    first,
    last,
    hold,
    caches,
    me_ref,
    own_ref,
    *refs,
):
    parts, _, width = own_ref.shape
    tail = 2 * cached_rows
    lines = own_ref.shape[1] - 2 * rows - tail
    heads = lines // rows
    here = lax.rem(me_ref[0], ring)
    scale = LOG2E / math.sqrt(width)
    refs = list(refs)

    def take(count):
        taken = refs[:count]
        del refs[:count]
        return taken

    pieces = [take(count) for count in counts]
    carried_caches = take(caches)
    carried = [] if first else take(3)
    if last:
        (out_ref,) = take(1)
    else:
        out_total, out_peak, out_sums = take(3)
    if hold:
        (out_cache,) = take(1)
    keys, values = refs

    sources = []
    for piece in pieces:
        if piece:
            sources.append([(ref, index, 0) for ref in piece for index in range(ref.shape[0])])
        else:
            sources.append([(own_ref, index, lines) for index in range(parts)])

    count = cached_rows * parts
    present = 0 if hold else count * len(steps) + sum(ref.shape[1] for ref in carried_caches)
    cached = -(-present // rows) * rows
    stretch = rows * len(steps)
    ones = jnp.ones((rows, width), jnp.bfloat16)
    for start in range(0, cached + parts * stretch, rows):
        values[start : start + rows, width:] = ones
    found = []
    for number, source in enumerate(sources):
        tails = []
        for part, (ref, index, base) in enumerate(source):
            place = cached + part * stretch + number * rows
            keys[place : place + rows, :] = ref[index, base : base + rows, :]
            values[place : place + rows, :width] = ref[index, base + rows : base + 2 * rows, :]
            tails.append(ref[index, base + 2 * rows : base + 2 * rows + tail, :].astype(jnp.float32))
        found.append(
            [
                jnp.concatenate([both[:cached_rows] for both in tails], 0).astype(jnp.bfloat16),
                jnp.concatenate([both[cached_rows:] for both in tails], 0).astype(jnp.bfloat16),
            ]
        )
    if hold:
        for number, pair in enumerate(found):
            for side in range(2):
                out_cache[side, number * count : (number + 1) * count, :] = pair[side]
    else:
        found += [(ref[0], ref[1]) for ref in carried_caches]
        place = 0
        for cache_keys, cache_values in found:
            size = cache_keys.shape[0]
            keys[place : place + size, :] = cache_keys
            values[place : place + size, :width] = cache_values
            place += size
        if place < cached:
            blank = jnp.zeros((cached - place, width), jnp.bfloat16)
            keys[place:cached, :] = blank
            values[place:cached, :width] = blank
    lane = lax.broadcasted_iota(jnp.int32, (1, rows), 1)
    edge = jnp.where(lane < present - (cached - rows), 0.0, LOW_SCORE)

    def fold(part, valid):
        query = own_ref[part, :lines, :]
        peak, total = None, None
        if not first:
            total = jnp.concatenate([carried[0][part], carried[2][part]], 1)
            peak = carried[1][part]
        full = cached + part * stretch
        chunks = split(0, full + valid * rows)
        if first:
            chunks = chunks[::-1]
        for low, high in chunks:
            scores = lax.dot_general(
                query, keys[low:high, :], NT, preferred_element_type=jnp.float32
            )
            tiles = []
            for spot in range(low, high, rows):
                tile = scores[:, spot - low : spot - low + rows] * scale
                if spot >= full and steps[(spot - full) // rows] == 0:
                    line = lax.broadcasted_iota(jnp.int32, (lines, rows), 0) % rows
                    column = lax.broadcasted_iota(jnp.int32, (lines, rows), 1)
                    tile = jnp.where(column <= line, tile, LOW_SCORE)
                elif spot == cached - rows and present < cached:
                    tile = tile + edge
                tiles.append(tile)
            top = jnp.max(functools.reduce(jnp.maximum, tiles), axis=1, keepdims=True)
            top = jnp.broadcast_to(top, (lines, width))
            if peak is not None:
                top = jnp.maximum(peak, top)
            weights = jnp.concatenate([jnp.exp2(tile - top) for tile in tiles], 1)
            added = lax.dot_general(
                weights.astype(jnp.bfloat16),
                values[low:high, :],
                NN,
                preferred_element_type=jnp.float32,
            )
            if peak is None:
                total = added
            else:
                fade = jnp.exp2(peak - top)
                total = total * jnp.concatenate([fade, fade], 1) + added
            peak = top
        if last:
            result = (total[:, :width] / total[:, width:]).astype(jnp.bfloat16)
            for head in range(heads):
                out_ref[part, :, head * width : (head + 1) * width] = result[
                    head * rows : (head + 1) * rows
                ]
        else:
            out_total[part] = total[:, :width]
            out_sums[part] = total[:, width:]
            out_peak[part] = peak

    if steps == (0,):
        for part in reversed(range(parts)):
            fold(part, 1)
        return
    owners = [lax.rem(here + step + ring, ring) for step in steps]
    earlier = sum((owner < here).astype(jnp.int32) for owner in owners)
    for valid in range(len(steps) + 1):

        @pl.when(earlier == valid)
        def _():
            for part in reversed(range(parts)):
                fold(part, valid)


def cross_kernel(
    slots,
    me_ref,
    start_ref,
    stop_ref,
    length_ref,
    gate_ref,
    query_ref,
    before_ref,
    own_ref,
    out_ref,
):
    rows = query_ref.shape[0]
    width = query_ref.shape[1]
    kv_heads = own_ref.shape[1]
    head_dim = own_ref.shape[2] // 2
    group = width // head_dim // kv_heads
    me = me_ref[0]
    before = jnp.maximum(me - 1, 0)
    before_stop = jnp.where(me > 0, stop_ref[before], 0)
    gate = jnp.tanh(jnp.full((rows, head_dim), gate_ref[0], jnp.float32))
    column = lax.broadcasted_iota(jnp.int32, (rows, 2 * slots), 1)
    line = lax.broadcasted_iota(jnp.int32, (rows, 2 * slots), 0) + me * rows
    late = column >= slots
    start = jnp.where(late, start_ref[me], start_ref[before])
    stop = jnp.where(late, stop_ref[me], before_stop)
    length = jnp.where(late, length_ref[me] + slots, length_ref[before])
    allowed = (start <= line) & (line < stop) & (column < length)
    scale = 1.0 / math.sqrt(head_dim)
    for kv_head in range(kv_heads):
        image = jnp.concatenate([before_ref[:, kv_head, :], own_ref[:, kv_head, :]], 0)
        image_keys = image[:, :head_dim]
        image_values = image[:, head_dim:]
        for member in range(group):
            spot = (kv_head * group + member) * head_dim
            query = query_ref[:, spot : spot + head_dim]
            scores = lax.dot_general(query, image_keys, NT, preferred_element_type=jnp.float32)
            scores = jnp.where(allowed, scores * scale, LOW_SCORE)
            highest = jnp.max(scores, axis=1, keepdims=True)
            weights = jnp.where(allowed, jnp.exp(scores - highest), 0.0)
            sums = jnp.sum(weights, axis=1, keepdims=True)
            sums = jnp.where(sums > 0.0, sums, 1.0)
            context = lax.dot_general(
                (weights / sums).astype(jnp.bfloat16),
                image_values,
                NN,
                preferred_element_type=jnp.float32,
            )
            out_ref[:, spot : spot + head_dim] = (gate * context).astype(jnp.bfloat16)


def shards(
    text_query,
    stretch_kv,
    cache_kv,
    cross_query,
    image_kv,
    image_start,
    image_stop,
    image_lengths,
    cross_gate,
):
    devices = lax.axis_size("seq")
    me = lax.axis_index("seq")
    rows, query_width = text_query.shape
    kv_heads = stretch_kv.shape[1]
    head_dim = stretch_kv.shape[2] // 2
    group = query_width // head_dim // kv_heads
    ring = devices // kv_heads
    cached_rows = cache_kv.shape[0]
    slots = image_kv.shape[1]
    columns = [[part * ring + spot for part in range(kv_heads)] for spot in range(ring)]

    def shift(values, step):
        pairs = [
            (part * ring + spot, part * ring + (spot + step) % ring)
            for part in range(kv_heads)
            for spot in range(ring)
        ]
        return lax.ppermute(values, "seq", pairs)

    vmem = pl.BlockSpec(memory_space=pltpu.VMEM)
    smem = pl.BlockSpec(memory_space=pltpu.SMEM)
    lines = group * rows
    message = pl.pallas_call(
        pack_kernel,
        out_shape=jax.ShapeDtypeStruct(
            (kv_heads, lines + 2 * rows + 2 * cached_rows, head_dim), jnp.bfloat16
        ),
        grid=(2,),
        in_specs=[
            pl.BlockSpec((rows, query_width // 2), lambda step: (0, step)),
            pl.BlockSpec(stretch_kv.shape, lambda step: (0, 0, 0)),
            pl.BlockSpec(cache_kv.shape, lambda step: (0, 0, 0)),
        ],
        out_specs=pl.BlockSpec(
            (kv_heads // 2, lines + 2 * rows + 2 * cached_rows, head_dim),
            lambda step: (step, 0, 0),
        ),
        scratch_shapes=[
            pltpu.VMEM((kv_heads, 2 * rows + 2 * cached_rows, head_dim), jnp.bfloat16)
        ],
        name="pack_message",
    )(text_query, stretch_kv, cache_kv)
    me_array = me.reshape(1).astype(jnp.int32)
    own_image = image_kv.reshape(image_kv.shape[1:])
    message, own_image = lax.optimization_barrier((message, own_image))
    image_before = lax.ppermute(own_image, "seq", [(i, i + 1) for i in range(devices - 1)])
    cross_context = pl.pallas_call(
        functools.partial(cross_kernel, slots),
        out_shape=jax.ShapeDtypeStruct(cross_query.shape, jnp.bfloat16),
        in_specs=[smem] * 5 + [vmem] * 3,
        out_specs=vmem,
        compiler_params=pltpu.CompilerParams(vmem_limit_bytes=16 * 2**20),
        cost_estimate=pl.CostEstimate(
            flops=400_000_000, bytes_accessed=1_200_000, transcendentals=200_000
        ),
        name="cross_attention",
    )(
        me_array,
        image_start,
        image_stop,
        image_lengths,
        cross_gate,
        cross_query,
        image_before,
        own_image,
    )

    arrived = lax.all_to_all(
        message, "seq", split_axis=0, concat_axis=0, axis_index_groups=columns, tiled=True
    )
    arrived, cross_context = lax.optimization_barrier((arrived, cross_context))

    def attend(steps, first, last, hold, caches, carried):
        pieces = [piece for step in steps for piece in arrivals[step]]
        count = kv_heads * cached_rows
        held = sum(cache.shape[1] for cache in caches) // count
        total_keys = kv_heads * len(steps) * rows
        if not hold:
            total_keys += -(-count * (len(steps) + held) // rows) * rows
        if last:
            out_shape = [jax.ShapeDtypeStruct((kv_heads, rows, group * head_dim), jnp.bfloat16)]
        else:
            out_shape = [jax.ShapeDtypeStruct((kv_heads, lines, head_dim), jnp.float32)] * 3
        if hold:
            out_shape.append(
                jax.ShapeDtypeStruct((2, count * len(steps), head_dim), jnp.bfloat16)
            )
        work = kv_heads * lines * len(steps) * rows * 3
        return pl.pallas_call(
            functools.partial(
                self_kernel,
                steps,
                tuple(len(arrivals[step]) for step in steps),
                rows,
                ring,
                cached_rows,
                first,
                last,
                hold,
                len(caches),
            ),
            out_shape=out_shape,
            in_specs=[smem] + [vmem] * (1 + len(pieces) + len(caches) + len(carried)),
            out_specs=[vmem] * len(out_shape),
            scratch_shapes=[
                pltpu.VMEM((total_keys, head_dim), jnp.bfloat16),
                pltpu.VMEM((total_keys, 2 * head_dim), jnp.bfloat16),
            ],
            compiler_params=pltpu.CompilerParams(vmem_limit_bytes=32 * 2**20),
            cost_estimate=pl.CostEstimate(
                flops=4 * work * head_dim, bytes_accessed=2_000_000, transcendentals=work
            ),
            name="self_attention",
        )(me_array, arrived, *pieces, *caches, *carried)

    up = down = arrived[:, lines:, :]
    arrivals = {0: ()}
    state, caches = (), ()
    steps = (0,)
    for step in range(1, ring // 2):
        down, up = shift(down, -1), shift(up, 1)
        *state, cache = attend(steps, step == 1, False, True, (), state)
        caches += (cache,)
        down, state = lax.optimization_barrier((down, state))
        arrivals[-step], arrivals[step] = (up,), (down,)
        steps = (-step, step)
    arrivals[ring // 2] = (shift(down, -1),)
    state = attend(steps, False, False, False, caches, state)
    (self_heads,) = attend((ring // 2,), False, True, False, (), state)

    returned = lax.all_to_all(
        self_heads, "seq", split_axis=0, concat_axis=0, axis_index_groups=columns, tiled=True
    )
    self_context = jnp.concatenate([returned[part] for part in range(kv_heads)], 1)
    return (self_context, cross_context)


def solution(mesh):
    in_specs = (
        P(("doc", "seq"), None),
        P(("doc", "seq"), None, None),
        P(("doc", "seq"), None, None),
        P(("doc", "seq"), None),
        P(("doc", "seq"), None, None, None),
        P("doc"),
        P("doc"),
        P("doc"),
        P("doc"),
    )
    out_specs = (P(("doc", "seq"), None), P(("doc", "seq"), None))
    return jax.shard_map(shards, mesh=mesh, in_specs=in_specs, out_specs=out_specs, check_vma=False)
```

```python
import functools
import math

import jax
import jax.numpy as jnp
from jax import lax
from jax.experimental import pallas as pl
from jax.experimental.pallas import tpu as pltpu
from jax.sharding import PartitionSpec as P

LOW_SCORE = -1e30
LOG2E = 1.4426950408889634
MOST_TILES = 8
NT = (((1,), (1,)), ((), ()))
NN = (((1,), (0,)), ((), ()))


def pack_kernel(query_ref, stretch_ref, cache_ref, out_ref, blocks):
    rows = query_ref.shape[0]
    parts, lines, width = out_ref.shape
    heads = query_ref.shape[1] // width // parts
    base = heads * rows
    step = pl.program_id(0)

    @pl.when(step == 0)
    def _():
        stretch = jnp.swapaxes(stretch_ref[...], 0, 1)
        blocks[:, :rows, :] = stretch[:, :, :width]
        blocks[:, rows : 2 * rows, :] = stretch[:, :, width:]
        cache = jnp.swapaxes(cache_ref[...].astype(jnp.float32), 0, 1)
        blocks[:, 2 * rows :, :] = jnp.concatenate(
            [cache[:, :, :width], cache[:, :, width:]], 1
        ).astype(jnp.bfloat16)

    for part in range(parts):
        for head in range(heads):
            spot = (part * heads + head) * width
            out_ref[part, head * rows : (head + 1) * rows, :] = query_ref[:, spot : spot + width]
    out_ref[:, base:lines, :] = blocks[pl.ds(step * parts, parts), :, :]


def split(low, high):
    tiles = (high - low) // 128
    count = -(-tiles // MOST_TILES)
    edges = [low + 128 * (tiles * number // count) for number in range(count)] + [high]
    return list(zip(edges[:-1], edges[1:]))


def self_kernel(
    steps,
    counts,
    rows,
    ring,
    cached_rows,
    first,
    last,
    hold,
    caches,
    me_ref,
    own_ref,
    *refs,
):
    parts, _, width = own_ref.shape
    tail = 2 * cached_rows
    lines = own_ref.shape[1] - 2 * rows - tail
    heads = lines // rows
    here = lax.rem(me_ref[0], ring)
    scale = LOG2E / math.sqrt(width)
    refs = list(refs)

    def take(count):
        taken = refs[:count]
        del refs[:count]
        return taken

    pieces = [take(count) for count in counts]
    carried_caches = take(caches)
    carried = [] if first else take(3)
    if last:
        (out_ref,) = take(1)
    else:
        out_total, out_peak, out_sums = take(3)
    if hold:
        (out_cache,) = take(1)
    keys, values = refs

    sources = []
    for piece in pieces:
        if piece:
            sources.append([(ref, index, 0) for ref in piece for index in range(ref.shape[0])])
        else:
            sources.append([(own_ref, index, lines) for index in range(parts)])

    count = cached_rows * parts
    present = 0 if hold else count * len(steps) + sum(ref.shape[1] for ref in carried_caches)
    cached = -(-present // rows) * rows
    stretch = rows * len(steps)
    ones = jnp.ones((rows, width), jnp.bfloat16)
    for start in range(0, cached + parts * stretch, rows):
        values[start : start + rows, width:] = ones
    found = []
    for number, source in enumerate(sources):
        tails = []
        for part, (ref, index, base) in enumerate(source):
            place = cached + part * stretch + number * rows
            keys[place : place + rows, :] = ref[index, base : base + rows, :]
            values[place : place + rows, :width] = ref[index, base + rows : base + 2 * rows, :]
            tails.append(ref[index, base + 2 * rows : base + 2 * rows + tail, :].astype(jnp.float32))
        found.append(
            [
                jnp.concatenate([both[:cached_rows] for both in tails], 0).astype(jnp.bfloat16),
                jnp.concatenate([both[cached_rows:] for both in tails], 0).astype(jnp.bfloat16),
            ]
        )
    if hold:
        for number, pair in enumerate(found):
            for side in range(2):
                out_cache[side, number * count : (number + 1) * count, :] = pair[side]
    else:
        found += [(ref[0], ref[1]) for ref in carried_caches]
        place = 0
        for cache_keys, cache_values in found:
            size = cache_keys.shape[0]
            keys[place : place + size, :] = cache_keys
            values[place : place + size, :width] = cache_values
            place += size
        if place < cached:
            blank = jnp.zeros((cached - place, width), jnp.bfloat16)
            keys[place:cached, :] = blank
            values[place:cached, :width] = blank
    lane = lax.broadcasted_iota(jnp.int32, (1, rows), 1)
    edge = jnp.where(lane < present - (cached - rows), 0.0, LOW_SCORE)

    def fold(part, valid):
        query = own_ref[part, :lines, :]
        peak, total = None, None
        if not first:
            total = jnp.concatenate([carried[0][part], carried[2][part]], 1)
            peak = carried[1][part]
        full = cached + part * stretch
        chunks = split(0, full + valid * rows)
        if first:
            chunks = chunks[::-1]
        for low, high in chunks:
            scores = lax.dot_general(
                query, keys[low:high, :], NT, preferred_element_type=jnp.float32
            )
            tiles = []
            for spot in range(low, high, rows):
                tile = scores[:, spot - low : spot - low + rows] * scale
                if spot >= full and steps[(spot - full) // rows] == 0:
                    line = lax.broadcasted_iota(jnp.int32, (lines, rows), 0) % rows
                    column = lax.broadcasted_iota(jnp.int32, (lines, rows), 1)
                    tile = jnp.where(column <= line, tile, LOW_SCORE)
                elif spot == cached - rows and present < cached:
                    tile = tile + edge
                tiles.append(tile)
            top = jnp.max(functools.reduce(jnp.maximum, tiles), axis=1, keepdims=True)
            top = jnp.broadcast_to(top, (lines, width))
            if peak is not None:
                top = jnp.maximum(peak, top)
            weights = jnp.concatenate([jnp.exp2(tile - top) for tile in tiles], 1)
            added = lax.dot_general(
                weights.astype(jnp.bfloat16),
                values[low:high, :],
                NN,
                preferred_element_type=jnp.float32,
            )
            if peak is None:
                total = added
            else:
                fade = jnp.exp2(peak - top)
                total = total * jnp.concatenate([fade, fade], 1) + added
            peak = top
        if last:
            share = pl.reciprocal(total[:, width:])
            result = (total[:, :width] * share).astype(jnp.bfloat16)
            for head in range(heads):
                out_ref[part, :, head * width : (head + 1) * width] = result[
                    head * rows : (head + 1) * rows
                ]
        else:
            out_total[part] = total[:, :width]
            out_sums[part] = total[:, width:]
            out_peak[part] = peak

    if steps == (0,):
        for part in reversed(range(parts)):
            fold(part, 1)
        return
    owners = [lax.rem(here + step + ring, ring) for step in steps]
    earlier = sum((owner < here).astype(jnp.int32) for owner in owners)
    for valid in range(len(steps) + 1):

        @pl.when(earlier == valid)
        def _():
            for part in reversed(range(parts)):
                fold(part, valid)


def cross_kernel(
    slots,
    me_ref,
    start_ref,
    stop_ref,
    length_ref,
    gate_ref,
    query_ref,
    before_ref,
    own_ref,
    out_ref,
):
    rows = query_ref.shape[0]
    width = query_ref.shape[1]
    kv_heads = own_ref.shape[1]
    head_dim = own_ref.shape[2] // 2
    group = width // head_dim // kv_heads
    me = me_ref[0]
    before = jnp.maximum(me - 1, 0)
    before_stop = jnp.where(me > 0, stop_ref[before], 0)
    gate = jnp.tanh(jnp.full((rows, head_dim), gate_ref[0], jnp.float32))
    column = lax.broadcasted_iota(jnp.int32, (rows, 2 * slots), 1)
    line = lax.broadcasted_iota(jnp.int32, (rows, 2 * slots), 0) + me * rows
    late = column >= slots
    start = jnp.where(late, start_ref[me], start_ref[before])
    stop = jnp.where(late, stop_ref[me], before_stop)
    length = jnp.where(late, length_ref[me] + slots, length_ref[before])
    allowed = (start <= line) & (line < stop) & (column < length)
    scale = 1.0 / math.sqrt(head_dim)
    for kv_head in range(kv_heads):
        image = jnp.concatenate([before_ref[:, kv_head, :], own_ref[:, kv_head, :]], 0)
        image_keys = image[:, :head_dim]
        image_values = image[:, head_dim:]
        for member in range(group):
            spot = (kv_head * group + member) * head_dim
            query = query_ref[:, spot : spot + head_dim]
            scores = lax.dot_general(query, image_keys, NT, preferred_element_type=jnp.float32)
            scores = jnp.where(allowed, scores * scale, LOW_SCORE)
            highest = jnp.max(scores, axis=1, keepdims=True)
            weights = jnp.where(allowed, jnp.exp(scores - highest), 0.0)
            sums = jnp.sum(weights, axis=1, keepdims=True)
            sums = jnp.where(sums > 0.0, sums, 1.0)
            context = lax.dot_general(
                (weights / sums).astype(jnp.bfloat16),
                image_values,
                NN,
                preferred_element_type=jnp.float32,
            )
            out_ref[:, spot : spot + head_dim] = (gate * context).astype(jnp.bfloat16)


def shards(
    text_query,
    stretch_kv,
    cache_kv,
    cross_query,
    image_kv,
    image_start,
    image_stop,
    image_lengths,
    cross_gate,
):
    devices = lax.axis_size("seq")
    me = lax.axis_index("seq")
    rows, query_width = text_query.shape
    kv_heads = stretch_kv.shape[1]
    head_dim = stretch_kv.shape[2] // 2
    group = query_width // head_dim // kv_heads
    ring = devices // kv_heads
    cached_rows = cache_kv.shape[0]
    slots = image_kv.shape[1]
    columns = [[part * ring + spot for part in range(kv_heads)] for spot in range(ring)]

    def shift(values, step):
        pairs = [
            (part * ring + spot, part * ring + (spot + step) % ring)
            for part in range(kv_heads)
            for spot in range(ring)
        ]
        return lax.ppermute(values, "seq", pairs)

    vmem = pl.BlockSpec(memory_space=pltpu.VMEM)
    smem = pl.BlockSpec(memory_space=pltpu.SMEM)
    lines = group * rows
    message = pl.pallas_call(
        pack_kernel,
        out_shape=jax.ShapeDtypeStruct(
            (kv_heads, lines + 2 * rows + 2 * cached_rows, head_dim), jnp.bfloat16
        ),
        grid=(2,),
        in_specs=[
            pl.BlockSpec((rows, query_width // 2), lambda step: (0, step)),
            pl.BlockSpec(stretch_kv.shape, lambda step: (0, 0, 0)),
            pl.BlockSpec(cache_kv.shape, lambda step: (0, 0, 0)),
        ],
        out_specs=pl.BlockSpec(
            (kv_heads // 2, lines + 2 * rows + 2 * cached_rows, head_dim),
            lambda step: (step, 0, 0),
        ),
        scratch_shapes=[
            pltpu.VMEM((kv_heads, 2 * rows + 2 * cached_rows, head_dim), jnp.bfloat16)
        ],
        name="pack_message",
    )(text_query, stretch_kv, cache_kv)
    me_array = me.reshape(1).astype(jnp.int32)
    own_image = image_kv.reshape(image_kv.shape[1:])
    message, own_image = lax.optimization_barrier((message, own_image))
    image_before = lax.ppermute(own_image, "seq", [(i, i + 1) for i in range(devices - 1)])
    cross_context = pl.pallas_call(
        functools.partial(cross_kernel, slots),
        out_shape=jax.ShapeDtypeStruct(cross_query.shape, jnp.bfloat16),
        in_specs=[smem] * 5 + [vmem] * 3,
        out_specs=vmem,
        compiler_params=pltpu.CompilerParams(vmem_limit_bytes=16 * 2**20),
        cost_estimate=pl.CostEstimate(
            flops=400_000_000, bytes_accessed=1_200_000, transcendentals=200_000
        ),
        name="cross_attention",
    )(
        me_array,
        image_start,
        image_stop,
        image_lengths,
        cross_gate,
        cross_query,
        image_before,
        own_image,
    )

    arrived = lax.all_to_all(
        message, "seq", split_axis=0, concat_axis=0, axis_index_groups=columns, tiled=True
    )
    arrived, cross_context = lax.optimization_barrier((arrived, cross_context))

    def attend(steps, first, last, hold, caches, carried):
        pieces = [piece for step in steps for piece in arrivals[step]]
        count = kv_heads * cached_rows
        held = sum(cache.shape[1] for cache in caches) // count
        total_keys = kv_heads * len(steps) * rows
        if not hold:
            total_keys += -(-count * (len(steps) + held) // rows) * rows
        if last:
            out_shape = [jax.ShapeDtypeStruct((kv_heads, rows, group * head_dim), jnp.bfloat16)]
        else:
            out_shape = [jax.ShapeDtypeStruct((kv_heads, lines, head_dim), jnp.float32)] * 3
        if hold:
            out_shape.append(
                jax.ShapeDtypeStruct((2, count * len(steps), head_dim), jnp.bfloat16)
            )
        work = kv_heads * lines * len(steps) * rows * 3
        return pl.pallas_call(
            functools.partial(
                self_kernel,
                steps,
                tuple(len(arrivals[step]) for step in steps),
                rows,
                ring,
                cached_rows,
                first,
                last,
                hold,
                len(caches),
            ),
            out_shape=out_shape,
            in_specs=[smem] + [vmem] * (1 + len(pieces) + len(caches) + len(carried)),
            out_specs=[vmem] * len(out_shape),
            scratch_shapes=[
                pltpu.VMEM((total_keys, head_dim), jnp.bfloat16),
                pltpu.VMEM((total_keys, 2 * head_dim), jnp.bfloat16),
            ],
            compiler_params=pltpu.CompilerParams(vmem_limit_bytes=32 * 2**20),
            cost_estimate=pl.CostEstimate(
                flops=4 * work * head_dim, bytes_accessed=2_000_000, transcendentals=work
            ),
            name="self_attention",
        )(me_array, arrived, *pieces, *caches, *carried)

    up = down = arrived[:, lines:, :]
    arrivals = {0: ()}
    state, caches = (), ()
    steps = (0,)
    for step in range(1, ring // 2):
        down, up = shift(down, -1), shift(up, 1)
        *state, cache = attend(steps, step == 1, False, True, (), state)
        caches += (cache,)
        down, state = lax.optimization_barrier((down, state))
        arrivals[-step], arrivals[step] = (up,), (down,)
        steps = (-step, step)
    arrivals[ring // 2] = (shift(down, -1),)
    state = attend(steps, False, False, False, caches, state)
    (self_heads,) = attend((ring // 2,), False, True, False, (), state)

    returned = lax.all_to_all(
        self_heads, "seq", split_axis=0, concat_axis=0, axis_index_groups=columns, tiled=True
    )
    self_context = jnp.concatenate([returned[part] for part in range(kv_heads)], 1)
    return (self_context, cross_context)


def solution(mesh):
    in_specs = (
        P(("doc", "seq"), None),
        P(("doc", "seq"), None, None),
        P(("doc", "seq"), None, None),
        P(("doc", "seq"), None),
        P(("doc", "seq"), None, None, None),
        P("doc"),
        P("doc"),
        P("doc"),
        P("doc"),
    )
    out_specs = (P(("doc", "seq"), None), P(("doc", "seq"), None))
    return jax.shard_map(shards, mesh=mesh, in_specs=in_specs, out_specs=out_specs, check_vma=False)
```
